128 devices in a mesh: dp: 8 (over x, core), row: 2 (over z_lo), col: 8 (over y, z_hi).
Axes of the slice: x: 4, y: 4, z: 4 (z_hi: 2, z_lo: 2; z = z_hi * 2 + z_lo), core: 2. Of those that a mesh axis runs over, the one named last changes fastest.
Arguments:
- tokens: bfloat16 [16384, 1024], P('dp', ('row', 'col')), may hold values from -12 to 12
- gain_attn: float32 [1024], P(('row', 'col')), may hold values from 0.5 to 1.5
- gain_moe: float32 [1024], P(('row', 'col')), may hold values from 0.5 to 1.5
- w_query: bfloat16 [1024, 1024], P('row', 'col'), may hold values from -0.75 to 0.75
- key_matrix: bfloat16 [1024, 512], P('row', 'col'), may hold values from -0.75 to 0.75
- value_matrix: bfloat16 [1024, 512], P('row', 'col'), may hold values from -0.1875 to 0.1875
- w_out: bfloat16 [1024, 1024], P('col', 'row'), may hold values from -6 to 6
- w_gate: bfloat16 [32, 1024, 512], P('col', None, 'row'), may hold values from -0.1875 to 0.1875
- w_up: bfloat16 [32, 1024, 512], P('col', None, 'row'), may hold values from -0.1875 to 0.1875
- w_down: bfloat16 [32, 512, 1024], P('col', 'row'), may hold values from -6 to 6
- routes: int32 [16384, 8], P('dp'), may hold values from 0 to 31, all different within a row; in each aligned block of 2048 rows (0 to 2047, 2048 to 4095, ...) at most 768 rows name the same one
- gate_weights: float32 [16384, 8], P('dp'), may hold values from 0.05 to 0.2
- segment_ids: int32 [8, 2048], P('dp'), may hold values from 0 to 3, never falling along the last dimension, each value on 1 to 1536 neighbouring positions
- cotangent: bfloat16 [16384, 1024], P('dp', ('row', 'col')), may hold values from -12 to 12
Outputs:
- result: bfloat16 [16384, 1024], P('dp', ('row', 'col'))
- grad_tokens: bfloat16 [16384, 1024], P('dp', ('row', 'col'))
- grad_gain_attn: float32 [1024], P(('row', 'col'))
- grad_gain_moe: float32 [1024], P(('row', 'col'))
- grad_query: float32 [1024, 1024], P('row', 'col')
- grad_key: float32 [1024, 512], P('row', 'col')
- grad_value: float32 [1024, 512], P('row', 'col')
- grad_out: float32 [1024, 1024], P('col', 'row')
- grad_gate: float32 [32, 1024, 512], P('col', None, 'row')
- grad_up: float32 [32, 1024, 512], P('col', None, 'row')
- grad_down: float32 [32, 512, 1024], P('col', 'row')
The draws below stay inside these ranges and needn't reach their ends.
Inputs may be any that keep to these rules, and one draw needn't show every extreme that they name: `routes`: each row names 8 different experts. Among the tokens of one sequence no expert is named more than 768 times, and in every draw some expert is named exactly 768 times in some sequence. `segment_ids`: along a sequence the numbers never fall; each document has 1 to 1536 tokens and one has exactly 1536.
All inputs are finite; a program needn't handle non-finite values.
Results may differ from the reference program's by a relative error of at most 0.029.
Values may be sent and summed in bfloat16 or wider, within the bound.
No kernel may reach another device: no remote copies, remote signals or barrier semaphores. Data moves between devices by JAX's collectives and lax.ppermute only.
A program may use at most 192 MiB of HBM per device.

```python
import math
import jax
import jax.numpy as jnp
import numpy as np
from jax import lax

MODEL_WIDTH = 1024
QUERY_HEAD_COUNT = 16
KEYVALUE_HEADS = 8
HEAD_FEATURES = 64
E = 32
FF = 512
TOPK = 8
SEQ = 2048
SEQS = 8
TOKENS = 16384
CAP = 768
DOCS = 4
LONGEST = 1536


def column_scale(count):
    return 3.0 ** (jnp.arange(count, dtype=jnp.float32) / (count - 1)) / 1.9


def draw_tokens(key, part):
    key = jax.random.fold_in(key, 11)
    col_scale = column_scale(MODEL_WIDTH)
    value_rows = jax.random.normal(key, (TOKENS, MODEL_WIDTH), jnp.float32) * col_scale
    return jnp.clip(value_rows, -12.0, 12.0).astype(jnp.bfloat16)


def draw_cotangent(key, part):
    key = jax.random.fold_in(key, 12)
    col_scale = column_scale(MODEL_WIDTH)
    value_rows = jax.random.normal(key, (TOKENS, MODEL_WIDTH), jnp.float32) * col_scale
    return jnp.clip(value_rows, -12.0, 12.0).astype(jnp.bfloat16)


def shard_levels(own_key, shape, cuts, smallest, largest):
    def one(position, blocks):
        draws = jax.random.uniform(jax.random.fold_in(jax.random.fold_in(own_key, 6), position), (blocks,), jnp.float32, smallest / len(cuts), largest / len(cuts))
        return jnp.repeat(jnp.exp(draws), shape[position] // blocks).reshape((-1,) + (1,) * (len(shape) - position - 1))

    gain = one(*cuts[0])
    for cut in cuts[1:]:
        gain = gain * one(*cut)
    return gain


def length_profile(number_of, total, most, slope):
    loads = [(1 << 20) // math.isqrt(standing ** slope) + 1 for standing in range(2, number_of + 1)]
    spare, given = total - most - (number_of - 1), [1] * (number_of - 1)
    while spare > 0:
        movable = [i for i in range(number_of - 1) if given[i] < most]
        pool, budget = sum([loads[i] for i in movable]), spare
        for i in movable:
            extra = min(most - given[i], max(1, budget * loads[i] // pool), spare)
            given[i] = given[i] + extra
            spare = spare - extra
    return np.array([most] + given)


def uneven(own_key, number_of, total, reach, skew):
    if number_of == 2:
        one = jax.random.randint(own_key, (), max(1, total - reach), min(reach, total - 1) + 1)
        return jnp.stack([one, total - one])
    lengths = jnp.asarray(length_profile(number_of, total, reach, skew), jnp.int32)
    pairs = (number_of - 1) // 2
    source_of, sink = lengths[1:1 + 2 * pairs:2], lengths[2:2 + 2 * pairs:2]
    slack = jnp.minimum(source_of - 1, reach - sink)
    moved = jax.random.randint(jax.random.fold_in(own_key, 1), (pairs,), 0, 1 << 20) % (slack + 1)
    lengths = lengths.at[1:1 + 2 * pairs:2].set(source_of - moved).at[2:2 + 2 * pairs:2].set(sink + moved)
    return lengths[jax.random.permutation(jax.random.fold_in(own_key, 2), number_of)]


def shared_out(stream_key, own, number, rows, number_of, top, reach, skew):
    order = jax.random.permutation(stream_key, number_of)
    heavy_load, usual = shares(number_of, rows * top, reach, skew, True), shares(number_of, rows * top, reach, skew, False)
    places = jnp.arange(number_of)

    def named(lengths, turn):
        used = int((lengths > 0).sum())
        fixed = max(1, used // 4)
        moved = fixed + (places - fixed + turn * (used - fixed)) % max(1, number_of - fixed)
        return jnp.zeros((number_of,), jnp.int32).at[order[jnp.where(places < fixed, places, moved)]].set(jnp.asarray(lengths, jnp.int32))

    lengths = jnp.where(number % 4 == 0, named(heavy_load, number // 4), named(usual, number - number // 4 - 1))
    mixed = jax.random.permutation(jax.random.fold_in(own, 3), number_of)
    source_of, taker = mixed[0:number_of // 2 * 2:2], mixed[1:number_of // 2 * 2:2]
    margin = jnp.minimum(lengths[source_of] - 1, reach - lengths[taker]) // 2
    margin = jnp.where((source_of == order[0]) | (taker == order[0]) | (lengths[taker] == 0), 0, jnp.maximum(margin, 0))
    moved = jax.random.randint(jax.random.fold_in(own, 4), (number_of // 2,), 0, 1 << 20) % (margin + 1)
    lengths = lengths.at[source_of].add(-moved).at[taker].add(moved)
    labels = jnp.searchsorted(jnp.cumsum(lengths), jnp.arange(rows * top), side="right").astype(jnp.int32)
    table = labels.reshape(top, rows).T
    table = table[jax.random.permutation(jax.random.fold_in(own, 1), rows)]
    turn = jax.random.randint(jax.random.fold_in(own, 2), (rows, 1), 0, top)
    return jnp.take_along_axis(table, (jnp.arange(top)[None, :] + turn) % top, axis=1)


def shares(number_of, total, most, lean, full):
    weights = [(1 << 20) // math.isqrt(standing ** lean) + 1 for standing in range(1, number_of + 1)]
    largest = most if full else min(most, max(-(-total // number_of), total * weights[0] // sum(weights)))
    least = 1 if total - largest >= number_of - 1 else 0
    counts, spare = [largest] + [least] * (number_of - 1), total - largest - least * (number_of - 1)
    while spare > 0:
        free = [i for i in range(1, number_of) if counts[i] < largest] or [i for i in range(1, number_of) if counts[i] < most]
        whole, budget = sum([weights[i] for i in free]), spare
        for i in free:
            extra = min(most - counts[i], max(1, budget * weights[i] // whole), spare)
            counts[i] = counts[i] + extra
            spare = spare - extra
    return np.array(counts)


def centred(own_key, extent, scale, bound, cuts=(), held_as=jnp.bfloat16):
    gain = shard_levels(own_key, extent, cuts, -0.22, 0.18) if cuts else 1.0
    entries = jax.random.normal(own_key, extent, jnp.float32) * scale * gain
    return jnp.minimum(jnp.maximum(entries, -bound), bound).astype(held_as)


def setup_inputs(seed: int = 0) -> dict:
    seeds = jax.random.split(jax.random.key(seed), 15)
    tokens = draw_tokens(jax.random.fold_in(seeds[14], 71), 0)
    gain_attn = jnp.clip(1.0 + 0.1 * jax.random.normal(seeds[1], (MODEL_WIDTH,), jnp.float32), 0.5, 1.5)
    gain_moe = jnp.clip(1.0 + 0.1 * jax.random.normal(seeds[2], (MODEL_WIDTH,), jnp.float32), 0.5, 1.5)
    w_query = centred(seeds[3], (MODEL_WIDTH, QUERY_HEAD_COUNT * HEAD_FEATURES), (MODEL_WIDTH // 16) ** -0.5, 0.75, ((0, 2), (1, 8)))
    key_matrix = centred(seeds[4], (MODEL_WIDTH, KEYVALUE_HEADS * HEAD_FEATURES), (MODEL_WIDTH // 16) ** -0.5, 0.75, ((0, 2), (1, 8)))
    value_matrix = centred(seeds[5], (MODEL_WIDTH, KEYVALUE_HEADS * HEAD_FEATURES), MODEL_WIDTH ** -0.5, 0.1875, ((0, 2), (1, 8)))
    w_out = centred(seeds[6], (QUERY_HEAD_COUNT * HEAD_FEATURES, MODEL_WIDTH), 1.0, 6.0, ((0, 8), (1, 2)))
    w_gate = centred(seeds[7], (E, MODEL_WIDTH, FF), MODEL_WIDTH ** -0.5, 0.1875, ((0, 8), (2, 2)))
    w_up = centred(seeds[8], (E, MODEL_WIDTH, FF), MODEL_WIDTH ** -0.5, 0.1875, ((0, 8), (2, 2)))
    w_down = centred(seeds[9], (E, FF, MODEL_WIDTH), 1.0, 6.0, ((0, 8), (1, 2)))
    routes_keys = jax.random.split(jax.random.fold_in(seeds[10], 1), TOKENS // SEQ)
    routes_turns = jax.random.permutation(jax.random.fold_in(seeds[10], 3), TOKENS // SEQ)
    routes = jax.vmap(lambda own, number: shared_out(jax.random.fold_in(seeds[10], 2), own, number, SEQ, E, TOPK, CAP, 1))(routes_keys, routes_turns).reshape((TOKENS, TOPK))
    gate_weights = jnp.clip(0.05 + 0.15 * jax.random.uniform(seeds[11], (TOKENS, TOPK), jnp.float32) ** shard_levels(seeds[11], (TOKENS, TOPK), ((0, 8),), -0.2, 0.2), 0.05, 0.2)
    segment_ids = jax.vmap(lambda own: jnp.searchsorted(jnp.cumsum(uneven(own, DOCS, SEQ, LONGEST, 1)), jnp.arange(SEQ), side="right"))(jax.random.split(seeds[12], SEQS)).reshape((SEQS, SEQ)).astype(jnp.int32)
    cotangent = draw_cotangent(jax.random.fold_in(seeds[14], 71), 0)
    return {"tokens": tokens, "gain_attn": gain_attn, "gain_moe": gain_moe, "w_query": w_query, "key_matrix": key_matrix, "value_matrix": value_matrix, "w_out": w_out, "w_gate": w_gate, "w_up": w_up, "w_down": w_down, "routes": routes, "gate_weights": gate_weights, "segment_ids": segment_ids, "cotangent": cotangent}


NORM_EPS = 1e-06
SCORE_SCALE = 0.015625
RESID_SCALE = 0.22
ROPE_BASE = 10000.0
MASKED_SCORE = -1e+30

@jax.custom_vjp
def lower_bound(v):
    return lax.optimization_barrier(v.astype(jnp.bfloat16)).astype(jnp.float32)

@jax.custom_vjp
def low_back(v):
    return v

def low_keep(v):
    return (lower_bound(v), None)

def low_pass(kept, grad):
    return (grad,)

def back_keep(v):
    return (v, None)

def back_low(kept, grad):
    return (lower_bound(grad),)
lower_bound.defvjp(low_keep, low_pass)
low_back.defvjp(back_keep, back_low)

def rotary(positions, width):
    middle = width // 2
    freq = ROPE_BASE ** (-2.0 * jnp.arange(middle, dtype=jnp.float32) / width)
    angle = positions.astype(jnp.float32)[:, None] * freq[None, :]
    cosine_table = jnp.concatenate([jnp.cos(angle), jnp.cos(angle)], axis=1)
    sine_values = jnp.concatenate([jnp.sin(angle), jnp.sin(angle)], axis=1)
    return (cosine_table, sine_values)

def rotate_pairs(value_rows, cosine_table, sine_values):
    middle = value_rows.shape[-1] // 2
    swapped = jnp.concatenate([-value_rows[..., middle:], value_rows[..., :middle]], axis=-1)
    return value_rows * cosine_table[:, None, :] + swapped * sine_values[:, None, :]

def rms_scale(value_rows):
    return lax.rsqrt(lax.optimization_barrier(jnp.mean(value_rows * value_rows, axis=-1, keepdims=True)) + NORM_EPS)

def dispatch(routes, gate_weights, first, count, capacity):
    sequence_length = routes.shape[0]
    experts = first + jnp.arange(count, dtype=jnp.int32)
    hits = routes[:, :, None] == experts[None, None, :]
    chosen = jnp.any(hits, axis=1)
    weight = lax.optimization_barrier(jnp.sum(jnp.where(hits, gate_weights[:, :, None], 0.0), axis=1))
    rank = (jnp.cumsum(chosen.astype(jnp.int32), axis=0) - 1).astype(jnp.int32)
    place = jnp.where(chosen, rank, capacity).astype(jnp.int32)
    column = jnp.broadcast_to(jnp.arange(count, dtype=jnp.int32)[None, :], place.shape)
    token_ids = jnp.broadcast_to(jnp.arange(sequence_length, dtype=jnp.int32)[:, None], place.shape)
    slots = jnp.full((count, capacity), sequence_length, jnp.int32).at[column, place].set(token_ids, mode='drop')
    slot_gate = jnp.zeros((count, capacity), jnp.float32).at[column, place].set(weight, mode='drop')
    return (slots, slot_gate)

def sequence_layer(params, inputs, segments, route, gate):
    gain_attn, gain_moe, w_query, key_matrix, value_matrix, w_out, w_gate, w_up, w_down = params
    sequence_length = inputs.shape[0]
    head_group = QUERY_HEAD_COUNT // KEYVALUE_HEADS
    highest = lax.Precision.HIGHEST
    normed_attn = inputs * rms_scale(inputs)
    hidden_attn = lower_bound(normed_attn * gain_attn)
    proj_query = low_back(jnp.dot(hidden_attn, w_query, precision=highest))
    key_projected = low_back(jnp.dot(hidden_attn, key_matrix, precision=highest))
    value_projected = low_back(jnp.dot(hidden_attn, value_matrix, precision=highest))
    positions = jnp.arange(sequence_length, dtype=jnp.int32)
    cosine_table, sine_values = rotary(positions, HEAD_FEATURES)
    query_rows = lower_bound(rotate_pairs(proj_query.reshape(sequence_length, QUERY_HEAD_COUNT, HEAD_FEATURES), cosine_table, sine_values))
    key_rows = lower_bound(rotate_pairs(key_projected.reshape(sequence_length, KEYVALUE_HEADS, HEAD_FEATURES), cosine_table, sine_values))
    value_rows = lower_bound(value_projected.reshape(sequence_length, KEYVALUE_HEADS, HEAD_FEATURES))
    allowed = (segments[:, None] == segments[None, :]) & (positions[:, None] >= positions[None, :])
    query_head_rows = query_rows.reshape(sequence_length, KEYVALUE_HEADS, head_group, HEAD_FEATURES).transpose(1, 0, 2, 3)
    key_heads = key_rows.transpose(1, 0, 2)
    value_heads = value_rows.transpose(1, 0, 2)

    def one_head(pieces):
        query_head, key_head, value_head = pieces
        score = low_back(jnp.einsum('qgd,kd->gqk', query_head, key_head, precision=highest) * SCORE_SCALE)
        masked = jnp.where(allowed[None], score, MASKED_SCORE)
        row_max = lax.optimization_barrier(jnp.max(masked, axis=-1, keepdims=True))
        weight = jnp.where(allowed[None], jnp.exp(masked - row_max), 0.0)
        prob = weight / lax.optimization_barrier(jnp.sum(weight, axis=-1, keepdims=True))
        return jnp.einsum('gqk,kd->qgd', lower_bound(prob), value_head, precision=highest)
    attended = lax.map(jax.checkpoint(one_head), (query_head_rows, key_heads, value_heads))
    heads_out = lower_bound(low_back(attended.transpose(1, 0, 2, 3).reshape(sequence_length, QUERY_HEAD_COUNT * HEAD_FEATURES)))
    branch = low_back(jnp.dot(heads_out, w_out, precision=highest))
    midway = inputs + RESID_SCALE * branch
    normed_moe = midway * rms_scale(midway)
    hidden_moe = lower_bound(normed_moe * gain_moe)
    slots, slot_gate = dispatch(route, gate, 0, E, CAP)
    padded = jnp.concatenate([hidden_moe, jnp.zeros((1, MODEL_WIDTH), jnp.float32)], axis=0)
    slot_rows = padded[slots]
    gate_pre = low_back(jnp.einsum('ecd,edf->ecf', slot_rows, w_gate, precision=highest))
    up_pre = low_back(jnp.einsum('ecd,edf->ecf', slot_rows, w_up, precision=highest))
    activated = lower_bound(jax.nn.silu(gate_pre) * up_pre)
    expert_out = low_back(jnp.einsum('ecf,efd->ecd', activated, w_down, precision=highest))
    weighted = (expert_out * slot_gate[:, :, None]).reshape(-1, MODEL_WIDTH)
    expert_sum = jnp.zeros((sequence_length + 1, MODEL_WIDTH), jnp.float32).at[slots.reshape(-1)].add(weighted)[:sequence_length]
    expert_sum = low_back(expert_sum)
    return midway + RESID_SCALE * expert_sum

def reference(tokens, gain_attn, gain_moe, w_query, key_matrix, value_matrix, w_out, w_gate, w_up, w_down, routes, gate_weights, segment_ids, cotangent):
    params = (gain_attn.astype(jnp.float32), gain_moe.astype(jnp.float32), w_query.astype(jnp.float32), key_matrix.astype(jnp.float32), value_matrix.astype(jnp.float32), w_out.astype(jnp.float32), w_gate.astype(jnp.float32), w_up.astype(jnp.float32), w_down.astype(jnp.float32))
    inputs_all = tokens.astype(jnp.float32).reshape(SEQS, SEQ, MODEL_WIDTH)
    routes_all = routes.reshape(SEQS, SEQ, TOPK)
    gates_all = gate_weights.astype(jnp.float32).reshape(SEQS, SEQ, TOPK)
    layer_step = jax.checkpoint(sequence_layer)

    def forward(weights, inputs_seq):

        def scan_body(carry, pieces):
            inputs, segments, route, gate = pieces
            return (carry, layer_step(weights, inputs, segments, route, gate))
        unused, outputs = lax.scan(scan_body, None, (inputs_seq, segment_ids, routes_all, gates_all))
        return outputs
    outputs, pullback = jax.vjp(forward, params, inputs_all)
    grads, grad_inputs = pullback(cotangent.astype(jnp.float32).reshape(SEQS, SEQ, MODEL_WIDTH))
    return (outputs.reshape(TOKENS, MODEL_WIDTH).astype(jnp.bfloat16), grad_inputs.reshape(TOKENS, MODEL_WIDTH).astype(jnp.bfloat16), grads[0], grads[1], grads[2], grads[3], grads[4], grads[5], grads[6], grads[7], grads[8])
```

```python
import functools

import jax
import jax.numpy as jnp
import numpy as np
from jax import lax
from jax.experimental import pallas as pl
from jax.experimental.pallas import tpu as pltpu
from jax.sharding import PartitionSpec as P

HEAD = 64
BLK = 256
NORM_EPS = 1e-06
SCORE_SCALE = 0.015625
RESID_SCALE = 0.22
ROPE_BASE = 10000.0
MASKED_SCORE = -1e30
EXTRA = 16
BF16 = jnp.bfloat16
F32 = jnp.float32
VMEM_LIMIT = 56 * 1024 * 1024

NN = (((1,), (0,)), ((), ()))
NT = (((1,), (1,)), ((), ()))


def dot(a, b, dims=NN):
    return lax.dot_general(a, b, dims, preferred_element_type=F32)


def params():
    return pltpu.CompilerParams(vmem_limit_bytes=VMEM_LIMIT)


def half_of(rows, which):
    size = rows.shape[0] // 8
    b = [rows[i * size : (i + 1) * size] for i in range(8)]
    return jnp.where(
        which == 0,
        jnp.concatenate([b[0], b[3], b[4], b[7]], axis=0),
        jnp.concatenate([b[1], b[2], b[5], b[6]], axis=0),
    )


def from_halves(first, second):
    size = first.shape[0] // 4
    f = [first[i * size : (i + 1) * size] for i in range(4)]
    s = [second[i * size : (i + 1) * size] for i in range(4)]
    return jnp.concatenate([f[0], s[0], s[1], f[1], f[2], s[2], s[3], f[3]], axis=0)


def natural(blocks):
    low = [b[:, :HEAD] for b in blocks]
    high = [b[:, HEAD:] for b in blocks]
    return jnp.concatenate(low + high, axis=1)


def to_blocks(low, high, index):
    part = slice(index * HEAD, (index + 1) * HEAD)
    return jnp.concatenate([low[:, part], high[:, part]], axis=1)


def swap_halves(rows):
    width = rows.shape[1]
    lane = lax.broadcasted_iota(jnp.int32, rows.shape, 1)
    ahead = pltpu.roll(rows, width - HEAD // 2, 1)
    behind = pltpu.roll(rows, HEAD // 2, 1)
    return jnp.where(lane % HEAD < HEAD // 2, ahead, behind)


TABLE_BLOCK, TABLE_FIRST, TABLE_PLACE, TABLE_TOKENS, TABLE_EXPERT = 0, 4, 8, 24, 32
DZ_ORDER = (0, 2, 1, 3)


def place_of(info_ref, dy, dz):
    return info_ref[TABLE_PLACE + 4 * dy + dz]


def fixed(shape):
    zeros = (0,) * len(shape)
    return pl.BlockSpec(shape, lambda i, s: zeros, pipeline_mode=pl.Buffered(1))


def pick_cols(info_ref, step, a_refs, b_refs, held):
    @pl.when(step == 0)
    def _():
        for dy, ref in enumerate(a_refs):
            for h in range(2):
                held[place_of(info_ref, dy, 2 * h)] = ref[h, : held.shape[1]]

    @pl.when(step == 1)
    def _():
        for h, ref in enumerate(b_refs):
            for dy in range(4):
                held[place_of(info_ref, dy, 2 * h)] = ref[dy]

    return natural([held[k] for k in range(held.shape[0])])


def pick_grid(info_ref, step, a_refs, b_refs, held):
    for index in range(4):
        p = index % 2

        @pl.when(step == index)
        def _():
            for dy in range(4):
                for h in range(2):
                    piece = a_refs[dy][2 * p + h] if index < 2 else b_refs[p + 2 * h][dy]
                    held[place_of(info_ref, dy, p + 2 * h)] = piece

    return natural([held[k] for k in range(held.shape[0])])


def token_rows_of(folded):
    total = jnp.sum(folded.T, axis=0, keepdims=True)
    parts = [total[:, k * 128 : (k + 1) * 128] for k in range(total.shape[1] // 128)]
    rows = jnp.concatenate(parts, axis=0)
    high = rows.astype(BF16).astype(F32)
    rest = jnp.zeros((EXTRA - 2 * rows.shape[0], 128), F32)
    return jnp.concatenate([high, rows - high, rest], axis=0).astype(BF16)


def fold_lanes(terms):
    folded = terms[:, :128]
    for k in range(1, terms.shape[1] // 128):
        folded = folded + terms[:, k * 128 : (k + 1) * 128]
    return folded


def turn(rows, cos, sin):
    return rows * cos + swap_halves(rows) * sin


def turn_half(rows, cos, sin):
    lane = lax.broadcasted_iota(jnp.int32, rows.shape, 1)
    return jnp.where(lane < HEAD, turn(rows, cos, sin), rows)


def angle_specs():
    def at(k):
        return pl.BlockSpec((BLK, 2 * HEAD), lambda i, s: (s[TABLE_BLOCK + 2 * i + k], 0))

    return [at(0), at(1), at(0), at(1)]


def angles(refs):
    cos = jnp.concatenate([refs[0][...], refs[1][...]], axis=0)
    sin = jnp.concatenate([refs[2][...], refs[3][...]], axis=0)
    return cos, sin


def project_kernel(info_ref, *refs):
    a_refs, b_refs = refs[:4], refs[4:6]
    w_ref = refs[6]
    q_ref, kv_ref, hid_ref, scale_ref, gain_out, held, few, gain_ref = refs[11:]
    step = pl.program_id(0)
    x = pick_cols(info_ref, step, a_refs, b_refs, held).astype(F32)

    @pl.when(step == 0)
    def _():
        for dy, ref in enumerate(a_refs):
            for h in range(2):
                few[place_of(info_ref, dy, 2 * h)] = ref[h, held.shape[1] :]
        rows = natural([few[k] for k in range(few.shape[0])]).astype(F32)
        gain_ref[...] = rows[0:1] + rows[1:2] + rows[2:3]
        gain_out[...] = rows[3:4] + rows[4:5] + rows[5:6]

    scale = lax.rsqrt(jnp.mean(x * x, axis=1, keepdims=True) + NORM_EPS)
    hidden = (x * scale * gain_ref[...]).astype(BF16)
    hid_ref[...] = hidden
    scale_ref[...] = jnp.broadcast_to(scale, scale_ref.shape)
    proj = dot(hidden, w_ref[...])
    cos, sin = angles(refs[7:11])
    width = q_ref.shape[1]
    q_ref[...] = turn(proj[:, :width], cos, sin).astype(BF16)
    kv_ref[...] = turn_half(proj[:, width:], cos, sin).astype(BF16)


def project(info, parts, weight, cos, sin):
    width, out = weight.shape
    tile, lanes = parts[-1].shape[1:]
    rows = 2 * tile

    def row_block(size):
        return pl.BlockSpec((tile, size), lambda i, s: (i, 0))

    return pl.pallas_call(
        project_kernel,
        grid_spec=pltpu.PrefetchScalarGridSpec(
            num_scalar_prefetch=1,
            grid=(2,),
            in_specs=[fixed(p.shape) for p in parts] + [fixed((width, out))] + angle_specs(),
            out_specs=[
                row_block(out // 2),
                row_block(out // 2),
                row_block(width),
                row_block(lanes),
                pl.BlockSpec((1, width), lambda i, s: (0, 0)),
            ],
            scratch_shapes=[
                pltpu.VMEM((width // lanes, tile, lanes), BF16),
                pltpu.VMEM((width // lanes, EXTRA, lanes), BF16),
                pltpu.VMEM((1, width), F32),
            ],
        ),
        out_shape=[
            jax.ShapeDtypeStruct((rows, out // 2), BF16),
            jax.ShapeDtypeStruct((rows, out // 2), BF16),
            jax.ShapeDtypeStruct((rows, width), BF16),
            jax.ShapeDtypeStruct((rows, lanes), F32),
            jax.ShapeDtypeStruct((1, width), F32),
        ],
        compiler_params=params(),
        cost_estimate=pl.CostEstimate(
            flops=2 * rows * width * out, bytes_accessed=16 * rows * width, transcendentals=0
        ),
        name="project",
    )(info, *parts, weight, cos, cos, sin, sin)


def key_offset(kb, half):
    return pl.multiple_of((kb + 1) // 2 % 2 * half + kb // 2 * BLK, BLK)


def stack_heads(rows):
    return jnp.concatenate([rows[:, :HEAD], rows[:, HEAD:]], axis=0)


def masked_scores(keys, queries, kb, qpos, qstart):
    scores = dot(keys, queries, NT) * SCORE_SCALE
    kpos = kb * BLK + lax.broadcasted_iota(jnp.int32, (BLK, 1), 0)
    allowed = (kpos <= qpos) & (kpos >= qstart)
    return jnp.where(allowed, scores, MASKED_SCORE)


def attend_kernel(
    info_ref, q_ref, kv_ref, start_ref, wo_ref, *refs, half
):
    a_refs, b_refs = refs[:4], refs[4:6]
    out_ref, lse_ref, keyval_t, held = refs[6:]
    step = pl.program_id(0)

    @pl.when(step == 0)
    def _():
        for k in range(kv_ref.shape[0] // BLK):
            rows = slice(k * BLK, (k + 1) * BLK)
            keyval_t[:, rows] = kv_ref[rows, :].astype(F32).T.astype(BF16)

    block = info_ref[TABLE_BLOCK + step]
    first = info_ref[TABLE_FIRST + step]
    queries = stack_heads(q_ref[...])
    position = block * BLK + lax.broadcasted_iota(jnp.int32, (1, BLK), 1)
    qpos = jnp.concatenate([position, position], axis=1)
    qstart = jnp.concatenate([start_ref[0], start_ref[0]], axis=1)

    def one(index, state):
        top, total, acc = state
        kb = block - index
        off = key_offset(kb, half)
        scores = masked_scores(kv_ref[pl.ds(off, BLK), :HEAD], queries, kb, qpos, qstart)
        new_top = jnp.maximum(top, jnp.max(scores, axis=0, keepdims=True))
        weight = jnp.exp(scores - new_top)
        alpha = jnp.exp(top - new_top)
        total = total * alpha + jnp.sum(weight, axis=0, keepdims=True)
        acc = acc * alpha + dot(keyval_t[HEAD:, pl.ds(off, BLK)], weight.astype(BF16))
        return (new_top, total, acc)

    both = 2 * BLK
    top, total, acc = lax.fori_loop(
        0,
        block - first + 1,
        one,
        (
            jnp.full((1, both), MASKED_SCORE, F32),
            jnp.zeros((1, both), F32),
            jnp.zeros((HEAD, both), F32),
        ),
    )
    heads = (acc / total).T
    heads = jnp.concatenate([heads[:BLK], heads[BLK:]], axis=1)
    out_ref[...] = heads
    lse_ref[0] = top + jnp.log(total)
    heads = heads.astype(BF16)
    low = dot(heads, wo_ref[0]).astype(BF16)
    high = dot(heads, wo_ref[1]).astype(BF16)
    for k in range(held.shape[0]):
        held[k] = to_blocks(low, high, k)

    @pl.when(step < 2)
    def _():
        for dy, ref in enumerate(a_refs):
            for h in range(2):
                ref[h] = held[place_of(info_ref, dy, 2 * h)]

    @pl.when(step >= 2)
    def _():
        for h, ref in enumerate(b_refs):
            for dy in range(4):
                ref[dy] = held[place_of(info_ref, dy, 2 * h)]


def attend(info, q, keyval, start, w_out):
    rows, width = q.shape
    steps = rows // BLK
    sequence = keyval.shape[0]
    half = w_out.shape[2]
    count = 2 * half // 128
    return pl.pallas_call(
        functools.partial(attend_kernel, half=sequence // 2),
        grid_spec=pltpu.PrefetchScalarGridSpec(
            num_scalar_prefetch=1,
            grid=(steps,),
            in_specs=[
                pl.BlockSpec((BLK, width), lambda i, s: (i, 0)),
                pl.BlockSpec((sequence, width), lambda i, s: (0, 0)),
                pl.BlockSpec((1, 1, BLK), lambda i, s: (i, 0, 0)),
                pl.BlockSpec((2, width, half), lambda i, s: (0, 0, 0)),
            ],
            out_specs=[
                pl.BlockSpec((2, BLK, 128), lambda i, s: (0, jnp.minimum(i, 1), 0))
                for _ in range(4)
            ]
            + [
                pl.BlockSpec((4, BLK, 128), lambda i, s: (0, jnp.maximum(i - 2, 0), 0))
                for _ in range(2)
            ]
            + [
                pl.BlockSpec((BLK, width), lambda i, s: (i, 0)),
                pl.BlockSpec((1, 1, 2 * BLK), lambda i, s: (i, 0, 0)),
            ],
            scratch_shapes=[
                pltpu.VMEM((width, sequence), BF16),
                pltpu.VMEM((count, BLK, 128), BF16),
            ],
        ),
        out_shape=[jax.ShapeDtypeStruct((2, rows // 2, 128), BF16) for _ in range(4)]
        + [jax.ShapeDtypeStruct((4, rows // 2, 128), BF16) for _ in range(2)]
        + [
            jax.ShapeDtypeStruct((rows, width), F32),
            jax.ShapeDtypeStruct((steps, 1, 2 * BLK), F32),
        ],
        compiler_params=params(),
        cost_estimate=pl.CostEstimate(
            flops=64 * rows * sequence * HEAD,
            bytes_accessed=32 * rows * sequence,
            transcendentals=rows * sequence,
        ),
        name="attend",
    )(info, q, keyval, start, w_out)


def attend_grad_kernel(
    info_ref, q_ref, kv_ref, start_ref, wo_ref, *refs, half
):
    a_refs, b_refs = refs[:4], refs[4:6]
    out_ref, lse_ref, dq_ref, dkv_ref, dwo_ref, keyval_t, held, branch_ref = refs[6:]
    step = pl.program_id(0)

    @pl.when(step == 0)
    def _():
        for k in range(kv_ref.shape[0] // BLK):
            rows = slice(k * BLK, (k + 1) * BLK)
            keyval_t[:, rows] = kv_ref[rows, :].astype(F32).T.astype(BF16)
        dkv_ref[...] = jnp.zeros_like(dkv_ref)
        dwo_ref[...] = jnp.zeros_like(dwo_ref)

    block = info_ref[TABLE_BLOCK + step]
    first = info_ref[TABLE_FIRST + step]
    queries = stack_heads(q_ref[...])
    heads = out_ref[...]
    for index in range(2):

        @pl.when(step == 2 * index)
        def _():
            whole = pick_cols(info_ref, jnp.int32(index), a_refs, b_refs, held)
            branch_ref[0] = whole[:BLK]
            branch_ref[1] = whole[BLK:]

    branch = branch_ref[step % 2]
    side = branch.shape[1] // 2
    grad_heads = (dot(branch[:, :side], wo_ref[0], NT) + dot(branch[:, side:], wo_ref[1], NT)).astype(
        BF16
    )
    dwo_ref[...] += dot(heads.T.astype(BF16), branch)
    grads = stack_heads(grad_heads)
    product = stack_heads(grad_heads.astype(F32) * heads)
    delta = jnp.sum(product.T, axis=0, keepdims=True)
    lse = lse_ref[0]
    position = block * BLK + lax.broadcasted_iota(jnp.int32, (1, BLK), 1)
    qpos = jnp.concatenate([position, position], axis=1)
    qstart = jnp.concatenate([start_ref[0], start_ref[0]], axis=1)

    def one(index, acc):
        kb = block - index
        off = key_offset(kb, half)
        place = pl.ds(off, BLK)
        scores = masked_scores(kv_ref[place, :HEAD], queries, kb, qpos, qstart)
        prob = jnp.exp(scores - lse)
        inner = dot(kv_ref[place, HEAD:], grads, NT)
        grad_score = (prob * (inner - delta)).astype(BF16)
        dk = dot(grad_score, queries) * SCORE_SCALE
        dv = dot(prob.astype(BF16), grads)
        dkv_ref[place, :] += jnp.concatenate([dk, dv], axis=1)
        return acc + dot(keyval_t[:HEAD, place], grad_score)

    acc = lax.fori_loop(0, block - first + 1, one, jnp.zeros((HEAD, 2 * BLK), F32))
    dq = acc.T * SCORE_SCALE
    dq_ref[...] = jnp.concatenate([dq[:BLK], dq[BLK:]], axis=1)


def attend_grad(info, q, keyval, start, w_out, parts, heads, lse):
    rows, width = q.shape
    steps = rows // BLK
    sequence = keyval.shape[0]
    half = w_out.shape[2]
    count = 2 * half // 128
    return pl.pallas_call(
        functools.partial(attend_grad_kernel, half=sequence // 2),
        grid_spec=pltpu.PrefetchScalarGridSpec(
            num_scalar_prefetch=1,
            grid=(steps,),
            in_specs=[
                pl.BlockSpec((BLK, width), lambda i, s: (i, 0)),
                pl.BlockSpec((sequence, width), lambda i, s: (0, 0)),
                pl.BlockSpec((1, 1, BLK), lambda i, s: (i, 0, 0)),
                pl.BlockSpec((2, width, half), lambda i, s: (0, 0, 0)),
            ]
            + [fixed(p.shape) for p in parts]
            + [
                pl.BlockSpec((BLK, width), lambda i, s: (i, 0)),
                pl.BlockSpec((1, 1, 2 * BLK), lambda i, s: (i, 0, 0)),
            ],
            out_specs=[
                pl.BlockSpec((BLK, width), lambda i, s: (i, 0)),
                pl.BlockSpec((sequence, width), lambda i, s: (0, 0)),
                pl.BlockSpec((width, 2 * half), lambda i, s: (0, 0)),
            ],
            scratch_shapes=[
                pltpu.VMEM((width, sequence), BF16),
                pltpu.VMEM((count, 2 * BLK, 128), BF16),
                pltpu.VMEM((2, BLK, 2 * half), BF16),
            ],
        ),
        out_shape=[
            jax.ShapeDtypeStruct((rows, width), F32),
            jax.ShapeDtypeStruct((sequence, width), F32),
            jax.ShapeDtypeStruct((width, 2 * half), F32),
        ],
        compiler_params=params(),
        cost_estimate=pl.CostEstimate(
            flops=64 * rows * sequence * HEAD,
            bytes_accessed=32 * rows * sequence,
            transcendentals=rows * sequence,
        ),
        name="attend_grad",
    )(info, q, keyval, start, w_out, *parts, heads, lse)


def send_grid(info_ref, step, low, high, extra, held, a_refs, b_refs):
    rows = low.shape[0]
    for k in range(held.shape[0]):
        held[k] = to_blocks(low, high, k)
    for index in range(4):
        p = index % 2

        @pl.when(step == index)
        def _():
            for dy in range(4):
                for h in range(2):
                    piece = held[place_of(info_ref, dy, p + 2 * h)]
                    ref, at = (a_refs[dy], h) if index < 2 else (b_refs[p + 2 * h], dy)
                    ref[at, :rows] = piece
                    ref[at, rows:] = extra


def pick_tall(info_ref, step, refs, held):
    size = held.shape[1]
    for index in range(4):
        p, rows = index % 2, slice(index // 2 * size, (index // 2 + 1) * size)

        @pl.when(step == index)
        def _():
            for dy in range(4):
                for h in range(2):
                    held[place_of(info_ref, dy, p + 2 * h)] = refs[p + 2 * h][dy, rows]

    return natural([held[k] for k in range(held.shape[0])])


def send_tall(info_ref, step, low, high, held, refs):
    size = held.shape[1]
    for k in range(held.shape[0]):
        held[k] = to_blocks(low, high, k)
    for index in range(4):
        p, rows = index % 2, slice(index // 2 * size, (index // 2 + 1) * size)

        @pl.when(step == index)
        def _():
            for dy in range(4):
                for h in range(2):
                    refs[p + 2 * h][dy, rows] = held[place_of(info_ref, dy, p + 2 * h)]


def send_grid_specs(rows, lanes):
    return [
        pl.BlockSpec((2, rows, lanes), lambda i, s: (jnp.minimum(i, 1), 0, 0)) for _ in range(4)
    ] + [pl.BlockSpec((4, rows, lanes), lambda i, s: (0, 0, 0)) for _ in range(4)]


def send_grid_shapes(rows, lanes):
    return [jax.ShapeDtypeStruct((4, rows, lanes), BF16) for _ in range(8)]


def gates_of(info_ref, refs, count):
    names = jnp.concatenate([refs[0][...], refs[1][...]], axis=1)
    weights = jnp.concatenate([refs[2][...], refs[3][...]], axis=1)
    first = info_ref[TABLE_EXPERT]
    gates = [
        jnp.sum(jnp.where(names == first + e, weights, 0.0), axis=0, keepdims=True)
        for e in range(count)
    ]
    return jnp.concatenate(gates + [jnp.zeros_like(gates[0])] * (8 - count), axis=0).T


def gate_specs(top, tile):
    def at(k):
        return pl.BlockSpec((top, tile // 2), lambda i, s: (0, s[TABLE_TOKENS + 2 * i + k]))

    return [at(0), at(1), at(0), at(1)]


def per_expert(experts, tile, hidden):
    return pl.BlockSpec((experts, tile, hidden), lambda i, s: (0, i, 0))


def experts_kernel(info_ref, *refs):
    gain_ref, wg_ref, wu_ref, wd_ref = refs[8:12]
    out_refs = refs[16:20]
    hid_ref, gate_ref, up_ref, h_ref, scale_ref, held = refs[20:]
    step = pl.program_id(0)
    x = pick_grid(info_ref, step, refs[:4], refs[4:8], held).astype(F32)
    scale = lax.rsqrt(jnp.mean(x * x, axis=1, keepdims=True) + NORM_EPS)
    hidden = (x * scale * gain_ref[...]).astype(BF16)
    hid_ref[...] = hidden
    scale_ref[...] = jnp.broadcast_to(scale, scale_ref.shape)
    gates = gates_of(info_ref, refs[12:16], wg_ref.shape[0])
    acted = []
    for e in range(wg_ref.shape[0]):
        gate_pre = dot(hidden, wg_ref[e])
        up_pre = dot(hidden, wu_ref[e])
        gate_ref[e] = gate_pre.astype(BF16)
        up_ref[e] = up_pre.astype(BF16)
        silu = gate_pre * (0.5 + 0.5 * jnp.tanh(0.5 * gate_pre))
        acted.append((silu * up_pre * gates[:, e : e + 1]).astype(BF16))
        h_ref[e] = acted[e]
    joined = jnp.concatenate(acted, axis=1)
    half = wd_ref.shape[1] // 2
    low = dot(joined, wd_ref[:, :half]).astype(BF16)
    high = dot(joined, wd_ref[:, half:]).astype(BF16)
    send_tall(info_ref, step, low, high, held, out_refs)


def experts_layer(info, parts, gain, w_gate, w_up, w_down, routes, weights):
    experts, width, hidden = w_gate.shape
    tile, lanes = parts[0].shape[1:]
    tokens = 4 * tile

    def per_expert_shape():
        return jax.ShapeDtypeStruct((experts, tokens, hidden), BF16)

    return pl.pallas_call(
        experts_kernel,
        grid_spec=pltpu.PrefetchScalarGridSpec(
            num_scalar_prefetch=1,
            grid=(4,),
            in_specs=[fixed(p.shape) for p in parts]
            + [
                fixed((1, width)),
                fixed((experts, width, hidden)),
                fixed((experts, width, hidden)),
                fixed((experts * hidden, width)),
            ]
            + gate_specs(routes.shape[0], tile),
            out_specs=[
                pl.BlockSpec((4, 2 * tile, lanes), lambda i, s: (0, 0, 0)) for _ in range(4)
            ]
            + [
                pl.BlockSpec((tile, width), lambda i, s: (i, 0)),
                per_expert(experts, tile, hidden),
                per_expert(experts, tile, hidden),
                per_expert(experts, tile, hidden),
                pl.BlockSpec((tile, lanes), lambda i, s: (i, 0)),
            ],
            scratch_shapes=[pltpu.VMEM((width // lanes, tile, lanes), BF16)],
        ),
        out_shape=[jax.ShapeDtypeStruct((4, 2 * tile, lanes), BF16) for _ in range(4)]
        + [
            jax.ShapeDtypeStruct((tokens, width), BF16),
            per_expert_shape(),
            per_expert_shape(),
            per_expert_shape(),
            jax.ShapeDtypeStruct((tokens, lanes), F32),
        ],
        compiler_params=params(),
        cost_estimate=pl.CostEstimate(
            flops=8 * tokens * width * experts * hidden,
            bytes_accessed=14 * tokens * width + 6 * width * experts * hidden,
            transcendentals=tokens * experts * hidden,
        ),
        name="experts",
    )(info, *parts, gain, w_gate, w_up, w_down, routes, routes, weights, weights)


def experts_grad_kernel(info_ref, *refs):
    wd_ref, wt_ref = refs[4:6]
    gate_ref, up_ref = refs[10:12]
    a_out, b_out = refs[12:16], refs[16:20]
    nat_ref, ggp_ref, gup_ref, held = refs[20:]
    step = pl.program_id(0)
    grad = pick_tall(info_ref, step, refs[:4], held)
    nat_ref[...] = grad
    gates = gates_of(info_ref, refs[6:10], wd_ref.shape[0])
    inner = jnp.zeros((grad.shape[0], 128), F32)
    pieces_gate, pieces_up = [], []
    for e in range(wd_ref.shape[0]):
        gate_pre = gate_ref[e].astype(F32)
        up_pre = up_ref[e].astype(F32)
        sig = 0.5 + 0.5 * jnp.tanh(0.5 * gate_pre)
        silu = gate_pre * sig
        grad_act = dot(grad, wd_ref[e], NT) * gates[:, e : e + 1]
        grad_gate = grad_act * up_pre * (sig + silu * (1.0 - sig))
        grad_up = grad_act * silu
        inner = inner + fold_lanes(grad_gate * gate_pre + grad_up * up_pre)
        grad_gate = grad_gate.astype(BF16)
        grad_up = grad_up.astype(BF16)
        ggp_ref[e] = grad_gate
        gup_ref[e] = grad_up
        pieces_gate.append(grad_gate)
        pieces_up.append(grad_up)
    joined = jnp.concatenate(pieces_gate + pieces_up, axis=1)
    half = wt_ref.shape[1] // 2
    low = dot(joined, wt_ref[:, :half]).astype(BF16)
    high = dot(joined, wt_ref[:, half:]).astype(BF16)
    send_grid(info_ref, step, low, high, token_rows_of(inner), held, a_out, b_out)


def experts_grad(info, parts, w_down, w_turned, routes, weights, gate_pre, up_pre):
    experts, hidden, width = w_down.shape
    tile, lanes = parts[0].shape[1:]
    tile = tile // 2
    tokens = 4 * tile

    def per_expert_shape():
        return jax.ShapeDtypeStruct((experts, tokens, hidden), BF16)

    return pl.pallas_call(
        experts_grad_kernel,
        grid_spec=pltpu.PrefetchScalarGridSpec(
            num_scalar_prefetch=1,
            grid=(4,),
            in_specs=[fixed(p.shape) for p in parts]
            + [fixed((experts, hidden, width)), fixed((2 * experts * hidden, width))]
            + gate_specs(routes.shape[0], tile)
            + [per_expert(experts, tile, hidden), per_expert(experts, tile, hidden)],
            out_specs=send_grid_specs(tile + EXTRA, lanes)
            + [
                pl.BlockSpec((tile, width), lambda i, s: (i, 0)),
                per_expert(experts, tile, hidden),
                per_expert(experts, tile, hidden),
            ],
            scratch_shapes=[pltpu.VMEM((width // lanes, tile, lanes), BF16)],
        ),
        out_shape=send_grid_shapes(tile + EXTRA, lanes)
        + [jax.ShapeDtypeStruct((tokens, width), BF16), per_expert_shape(), per_expert_shape()],
        compiler_params=params(),
        cost_estimate=pl.CostEstimate(
            flops=8 * tokens * width * experts * hidden,
            bytes_accessed=16 * tokens * width + 6 * width * experts * hidden,
            transcendentals=tokens * experts * hidden,
        ),
        name="experts_grad",
    )(info, *parts, w_down, w_turned, routes, routes, weights, weights, gate_pre, up_pre)


def weight_grads_kernel(rows_ref, grad_ref, gate_ref, up_ref, h_ref, out_ref, turned):
    @pl.when(pl.program_id(0) == 0)
    def _():
        for k in range(rows_ref.shape[0] // 512):
            part = slice(k * 512, (k + 1) * 512)
            turned[:, part] = rows_ref[part, :].T

    size = out_ref.shape[3]
    gate = dot(turned[...], gate_ref[0]).astype(BF16)
    up = dot(turned[...], up_ref[0]).astype(BF16)
    down = dot(h_ref[0].T, grad_ref[...]).astype(BF16)
    side = down.shape[0]
    for k in range(out_ref.shape[0]):
        rows = slice(k * size, (k + 1) * size)
        out_ref[k, 0, 0] = gate[rows]
        out_ref[k, 0, 1] = up[rows]
        at, lane = k * size % side, k * size // side * side
        out_ref[k, 0, 2] = down[at : at + size, lane : lane + side]


def weight_grads(rows, grad, grad_gate, grad_up, h, shards):
    tokens, width = rows.shape
    experts, _, hidden = grad_gate.shape
    size = width // shards

    def per_expert():
        return pl.BlockSpec((1, tokens, hidden), lambda i: (i, 0, 0))

    def whole():
        return pl.BlockSpec((tokens, width), lambda i: (0, 0), pipeline_mode=pl.Buffered(1))

    return pl.pallas_call(
        weight_grads_kernel,
        grid=(experts,),
        in_specs=[whole(), whole(), per_expert(), per_expert(), per_expert()],
        out_specs=pl.BlockSpec((shards, 1, 3, size, hidden), lambda i: (0, i, 0, 0, 0)),
        out_shape=jax.ShapeDtypeStruct((shards, experts, 3, size, hidden), BF16),
        scratch_shapes=[pltpu.VMEM((width, tokens), BF16)],
        compiler_params=params(),
        cost_estimate=pl.CostEstimate(
            flops=6 * tokens * width * experts * hidden,
            bytes_accessed=4 * tokens * width + 6 * experts * hidden * (tokens + width),
            transcendentals=0,
        ),
        name="weight_grads",
    )(rows, grad, grad_gate, grad_up, h)


def spread_kernel(in_ref, gate_ref, up_ref, down_ref):
    size = in_ref.shape[3]
    side = down_ref.shape[1]
    for k in range(in_ref.shape[0]):
        rows = slice(k * size, (k + 1) * size)
        gate_ref[0, rows] = in_ref[k, 0, 0].astype(F32)
        up_ref[0, rows] = in_ref[k, 0, 1].astype(F32)
        at, lane = k * size % side, k * size // side * side
        down_ref[0, at : at + size, lane : lane + side] = in_ref[k, 0, 2].astype(F32)


def spread(value):
    shards, experts, _, size, hidden = value.shape
    width = shards * size
    return pl.pallas_call(
        spread_kernel,
        grid=(experts,),
        in_specs=[pl.BlockSpec((shards, 1, 3, size, hidden), lambda i: (0, i, 0, 0, 0))],
        out_specs=[
            pl.BlockSpec((1, width, hidden), lambda i: (i, 0, 0)),
            pl.BlockSpec((1, width, hidden), lambda i: (i, 0, 0)),
            pl.BlockSpec((1, hidden, width), lambda i: (i, 0, 0)),
        ],
        out_shape=[
            jax.ShapeDtypeStruct((experts, width, hidden), F32),
            jax.ShapeDtypeStruct((experts, width, hidden), F32),
            jax.ShapeDtypeStruct((experts, hidden, width), F32),
        ],
        compiler_params=params(),
        cost_estimate=pl.CostEstimate(
            flops=0, bytes_accessed=18 * experts * width * hidden, transcendentals=0
        ),
        name="spread",
    )(value)


def hidden_grad_kernel(info_ref, dq_ref, dkv_ref, got_ref, q_ref, kv_ref, *refs):
    w_ref, a_refs, b_refs, gp_ref, held = refs[4], refs[5:9], refs[9:11], refs[11], refs[12]
    step = pl.program_id(0)
    rows = dq_ref.shape[0]
    dkv = dkv_ref[...] + got_ref[...].astype(F32)
    grad = jnp.concatenate([dq_ref[...], dkv], axis=1)
    value = jnp.concatenate([q_ref[...], kv_ref[...]], axis=1).astype(F32)
    extra = token_rows_of(fold_lanes(grad * value))
    cos, sin = angles(refs[:4])
    width = dq_ref.shape[1]
    turned = [turn(grad[:, :width], cos, -sin), turn_half(grad[:, width:], cos, -sin)]
    turned = jnp.concatenate(turned, axis=1).astype(BF16)
    gp_ref[...] = turned
    half = w_ref.shape[0] // 2
    low = dot(turned, w_ref[:half, :], NT).astype(BF16)
    high = dot(turned, w_ref[half:, :], NT).astype(BF16)
    for k in range(held.shape[0]):
        held[k] = to_blocks(low, high, k)
    for index in range(2):

        @pl.when(step == index)
        def _():
            for dy in range(4):
                for h in range(2):
                    ref, at = (a_refs[dy], h) if index == 0 else (b_refs[h], dy)
                    ref[at, :rows] = held[place_of(info_ref, dy, 2 * h)]
                    ref[at, rows:] = extra


def hidden_grad(info, dq, dkv, got, q, kv, cos, sin, weight, lanes):
    rows, width = dq.shape
    features, out = weight.shape
    tile = rows // 2
    tall = tile + EXTRA

    def row_block(size):
        return pl.BlockSpec((tile, size), lambda i, s: (i, 0))

    return pl.pallas_call(
        hidden_grad_kernel,
        grid_spec=pltpu.PrefetchScalarGridSpec(
            num_scalar_prefetch=1,
            grid=(2,),
            in_specs=[row_block(width) for _ in range(5)]
            + angle_specs()
            + [fixed((features, out))],
            out_specs=[pl.BlockSpec((2, tall, lanes), lambda i, s: (0, 0, 0)) for _ in range(4)]
            + [pl.BlockSpec((4, tall, lanes), lambda i, s: (0, 0, 0)) for _ in range(2)]
            + [row_block(out)],
            scratch_shapes=[pltpu.VMEM((features // lanes, tile, lanes), BF16)],
        ),
        out_shape=[jax.ShapeDtypeStruct((2, tall, lanes), BF16) for _ in range(4)]
        + [jax.ShapeDtypeStruct((4, tall, lanes), BF16) for _ in range(2)]
        + [jax.ShapeDtypeStruct((rows, out), BF16)],
        compiler_params=params(),
        cost_estimate=pl.CostEstimate(
            flops=2 * rows * features * out,
            bytes_accessed=16 * rows * features,
            transcendentals=0,
        ),
        name="hidden_grad",
    )(info, dq, dkv, got, q, kv, cos, cos, sin, sin, weight)


def fold_back(rows):
    side = rows.shape[1] // 2
    return jnp.concatenate([rows[:, :side], rows[:, side:]], axis=0)


def unfold_back(rows):
    side = rows.shape[0] // 2
    return jnp.concatenate([rows[:side], rows[side:]], axis=1)


def rotary_tables(sequence):
    freq = np.float32(ROPE_BASE) ** (-np.arange(0, HEAD, 2, dtype=np.float32) / np.float32(HEAD))
    angle = np.arange(sequence, dtype=np.float32)[:, None] * freq[None, :]
    angle = angle.astype(np.float64)
    cosine, sine = np.cos(angle).astype(np.float32), np.sin(angle).astype(np.float32)
    cos = np.concatenate([cosine] * 4, axis=1)
    sin = np.concatenate([-sine, sine] * 2, axis=1)
    return jnp.asarray(cos), jnp.asarray(sin)


def body(
    tokens,
    gain_attn,
    gain_moe,
    w_query,
    key_matrix,
    value_matrix,
    w_out,
    w_gate,
    w_up,
    w_down,
    routes,
    gate_weights,
    segment_ids,
    cotangent,
    *,
    cols,
    shards,
):
    sequence = tokens.shape[0]
    half = sequence // 2
    quarter = sequence // 4
    features = w_gate.shape[1]
    experts, _, hidden = w_gate.shape
    lanes = 2 * HEAD
    row = lax.axis_index("row")
    col = lax.axis_index("col")
    grid = ("row", "col")
    y = col // 2
    z = (col % 2) * 2 + row
    lower = row == 0

    def linear(py, pz):
        return (pz % 2) * cols + (py % 4) * 2 + (pz % 4) // 2

    def fetch(value, dy, dz):
        pairs = [(linear(a + dy, b + dz), linear(a, b)) for a in range(4) for b in range(4)]
        return lax.ppermute(value, grid, pairs)

    def send(value, dy, dz):
        return fetch(value, -dy % 4, -dz % 4)

    def exchange(value):
        return lax.ppermute(value, "row", [(0, 1), (1, 0)])

    def widen(own, other):
        return jnp.where(
            lower, jnp.concatenate([own, other], axis=1), jnp.concatenate([other, own], axis=1)
        )

    together = lax.optimization_barrier

    def gather_cols(value, extra=None, beside=None, beside_next=None):
        size = half // 2
        first, second = value[:size], value[size:half]
        if extra is not None:
            first = jnp.concatenate([first, extra], axis=0)
        got = [fetch(first, 0, 2)] + [fetch(second, dy, 0) for dy in (2, 1, 3)]
        got, beside = together((got, beside))
        a = jnp.stack([first, got[0]])
        b = jnp.stack([second, got[2], got[1], got[3]])
        got = [fetch(b, 0, 2)] + [fetch(a, dy, 0) for dy in (2, 1, 3)]
        got, beside_next = together((got, beside_next))
        return [a, got[2], got[1], got[3], b, got[0]], beside, beside_next

    def gather_grid(value):
        size = half // 2
        first, second = value[:size], value[size:]
        got = [fetch(first, 0, dz) for dz in (2, 1, 3)] + [fetch(second, dy, 0) for dy in (2, 1, 3)]
        got = together(got)
        a = jnp.stack([first, *got[:3]])
        b = jnp.stack([second, got[4], got[3], got[5]])
        got = together(
            [fetch(a, dy, 0) for dy in (2, 1, 3)] + [fetch(b, 0, dz) for dz in (2, 1, 3)]
        )
        return [a, got[1], got[0], got[2], b, got[4], got[3], got[5]]

    def total(values):
        out = values[0].astype(F32)
        for value in values[1:]:
            out = out + value.astype(F32)
        return out

    def scatter_cols_start(parts):
        return [send(parts[5], 0, 2)] + [send(parts[dy], dy, 0) for dy in (2, 1, 3)]

    def scatter_cols_next(parts, got):
        a, b = total([parts[0], *got[1:]]), total([parts[4], got[0]])
        sent = [send(a[1].astype(BF16), 0, 2)] + [
            send(b[dy].astype(BF16), dy, 0) for dy in (2, 1, 3)
        ]
        return [a[0], b[0]], sent

    def scatter_cols_end(kept, got):
        return total([kept[0], got[0]]), total([kept[1], *got[1:]])

    def scatter_grid_start(parts):
        return [send(parts[dy], dy, 0) for dy in (2, 1, 3)] + [
            send(parts[4 + dz], 0, dz) for dz in (2, 1, 3)
        ]

    def scatter_grid_next(parts, got):
        a, b = total([parts[0], *got[:3]]), total([parts[4], *got[3:]])
        sent = [send(a[i].astype(BF16), 0, DZ_ORDER[i]) for i in (1, 2, 3)] + [
            send(b[dy].astype(BF16), dy, 0) for dy in (2, 1, 3)
        ]
        return [a[0], b[0]], sent

    def scatter_grid_end(kept, got):
        return total([kept[0], *got[:3]]), total([kept[1], *got[3:]])

    def token_sums(a, b):
        pieces = []
        for part in (a, b):
            count = quarter // 128
            rows = part[quarter : quarter + count] + part[quarter + count : quarter + 2 * count]
            pieces.append(rows.reshape(quarter, 1))
        return jnp.concatenate(pieces, axis=0)

    def rows_of(a, b):
        return jnp.concatenate([a[:quarter], b[:quarter]], axis=0)

    def fold_rows(value, count):
        size = value.shape[0] // count
        return jnp.concatenate([value[k * size : (k + 1) * size] for k in range(count)], axis=1)

    def unfold_rows(value, count):
        size = value.shape[1] // count
        return jnp.concatenate([value[:, k * size : (k + 1) * size] for k in range(count)], axis=0)

    def in_parts(gain):
        high = lax.reduce_precision(gain, 8, 7)
        middle = lax.reduce_precision(gain - high, 8, 7)
        return [high, middle, gain - high - middle]

    gain_rows = jnp.stack(in_parts(gain_attn) + in_parts(gain_moe)).astype(BF16)
    gain_rows = jnp.concatenate([gain_rows, jnp.zeros((EXTRA - 6, HEAD), BF16)], axis=0)

    other = jnp.concatenate([half_of(tokens, 1 - row), gain_rows], axis=0)
    got = exchange(other)
    token_rows = widen(jnp.concatenate([half_of(tokens, row), gain_rows], axis=0), got)
    token_rows, gain_rows = token_rows[:half], token_rows[half:]
    token_rows, segment_ids, w_query, w_out, cotangent = together(
        (token_rows, segment_ids, w_query, w_out, cotangent)
    )

    joined_own = jnp.concatenate([w_query, key_matrix, value_matrix], axis=1)
    cot_other = half_of(cotangent, 1 - row)
    packed = jnp.concatenate([joined_own, fold_back(w_out), fold_rows(cot_other, 4)], axis=0)

    segments = segment_ids[0]
    before = [jnp.sum((segments < v).astype(jnp.int32)) for v in range(4)]
    start = jnp.where(
        segments == 0,
        before[0],
        jnp.where(segments == 1, before[1], jnp.where(segments == 2, before[2], before[3])),
    )
    own_start = half_of(start, row)
    index = jnp.arange(half // BLK, dtype=jnp.int32)
    block_ids = 2 * index + jnp.where(index % 2 == 0, row, 1 - row)
    start_rows = own_start.reshape(half // BLK, 1, BLK)
    other_ids = 2 * index + jnp.where(index % 2 == 0, 1 - row, row)
    step_blocks = jnp.concatenate([block_ids[:2], other_ids[:2], block_ids[2:], other_ids[2:]])
    index = jnp.arange(16, dtype=jnp.int32)
    places = (y + index // 4) % 4 * 2 + (z + index % 4) % 4 // 2
    info = jnp.concatenate(
        [block_ids, own_start[::BLK] // BLK, places, step_blocks, (col * experts).reshape(1)]
    ).astype(jnp.int32)
    token_parts, _, got = gather_cols(token_rows, gain_rows, None, exchange(packed))
    middle = joined_own.shape[0]
    last = middle + 2 * w_out.shape[0]
    joined_other, w_out_other = got[:middle], unfold_back(got[middle:last])
    cot_rows = widen(half_of(cotangent, row), unfold_rows(got[last:], 4))
    joined = jnp.where(
        lower,
        jnp.concatenate([joined_own, joined_other], axis=0),
        jnp.concatenate([joined_other, joined_own], axis=0),
    )
    w_out_full = jnp.where(lower, jnp.stack([w_out, w_out_other]), jnp.stack([w_out_other, w_out]))
    cos, sin = rotary_tables(sequence)
    token_parts, joined, info = together((token_parts, joined, info))

    cot = (RESID_SCALE * cot_rows.astype(F32)).astype(BF16)
    got = [fetch(cot, dy, 0) for dy in (2, 1, 3)]
    q, kv, hidden_attn, scale_attn, gain_full = project(info, token_parts, joined, cos, sin)
    got, q, kv = together((got, q, kv))
    kv_other = exchange(kv)
    cot = jnp.stack([cot, got[1], got[0], got[2]])
    keyval = jnp.where(
        lower,
        jnp.concatenate([kv, kv_other], axis=0),
        jnp.concatenate([kv_other, kv], axis=0),
    )
    far = fetch(cot, 0, 2)
    *parts, heads, lse = attend(info, q, keyval, start_rows, w_out_full)
    far, parts, w_gate, w_up = together((far, parts, w_gate, w_up))
    w_turned = jnp.concatenate(
        [
            jnp.swapaxes(w_gate, 1, 2).reshape(experts * hidden, features),
            jnp.swapaxes(w_up, 1, 2).reshape(experts * hidden, features),
        ],
        axis=0,
    )
    got = together(scatter_cols_start(parts))
    kept, got = scatter_cols_next(parts, got)
    branch = jnp.concatenate(scatter_cols_end(kept, together(got)), axis=0)
    inputs = token_rows.astype(F32)
    midway = inputs + RESID_SCALE * branch
    mid_parts = gather_grid(midway.astype(BF16))
    mid_parts, cot = together((mid_parts, cot))
    near = [fetch(cot, 0, dz) for dz in (1, 3)]
    route_rows, weight_rows = routes.T, gate_weights.T
    outs = experts_layer(
        info,
        mid_parts,
        gain_full,
        w_gate,
        w_up,
        w_down.reshape(experts * hidden, features),
        route_rows,
        weight_rows,
    )
    out_parts, (hidden_moe, gate_pre, up_pre, acted, scale_all) = outs[:4], outs[4:]
    near, out_parts, gate_pre = together((near, out_parts, gate_pre))
    cot_parts = [cot, near[0], far, near[1]]

    out_near = [send(out_parts[dz], 0, dz) for dz in (1, 3)]
    outs = experts_grad(
        info, cot_parts, w_down, w_turned, route_rows, weight_rows, gate_pre, up_pre
    )
    out_near, outs = together((out_near, outs))
    parts, (grad_nat, ggp, gup) = outs[:8], outs[8:]
    got = scatter_grid_start(parts)
    weights = weight_grads(hidden_moe, grad_nat, ggp, gup, acted, shards)
    got, weights = together((got, weights))
    weights = lax.psum_scatter(weights, "dp", scatter_dimension=0, tiled=True)
    kept, got = scatter_grid_next(parts, got)
    got = together(got)
    sum_a, sum_b = scatter_grid_end(kept, got)

    own_gains = gain_rows[:6].astype(F32)
    own_gains = [
        own_gains[0] + own_gains[1] + own_gains[2],
        own_gains[3] + own_gains[4] + own_gains[5],
    ]
    scale_moe = jnp.concatenate([scale_all[:quarter], scale_all[half : half + quarter]], axis=0)
    own_inner = token_sums(sum_a, sum_b) / features
    grad_hidden = rows_of(sum_a, sum_b)
    normed_moe = midway * scale_moe
    gain_moe_part = jnp.sum(grad_hidden * normed_moe, axis=0)
    grad_mid = cot_rows.astype(F32) + scale_moe * (
        grad_hidden * own_gains[1][None, :] - normed_moe * own_inner
    )
    branch_parts, _, _ = gather_cols((RESID_SCALE * grad_mid).astype(BF16))
    branch_parts, out_parts = together((branch_parts, out_parts))
    out_far = send(out_parts[2], 0, 2)
    dq, dkv, dwo = attend_grad(info, q, keyval, start_rows, w_out_full, branch_parts, heads, lse)
    out_far, dkv, weights = together((out_far, dkv, weights))
    weights = lax.all_gather(weights, "dp", axis=0, tiled=True)
    mine = jnp.where(lower, dkv[:half], dkv[half:])
    theirs = exchange(jnp.where(lower, dkv[half:], dkv[:half]).astype(BF16))
    out_sum = total([out_parts[0], *out_near, out_far])
    out_got = [send(out_sum[dy].astype(BF16), dy, 0) for dy in (2, 1, 3)]
    *parts, grad_proj = hidden_grad(info, dq, mine, theirs, q, kv, cos, sin, joined, lanes)
    out_got, parts = together((out_got, parts))
    expert_sum = total([out_sum[0], *out_got])

    def over_dp(value, change):
        return lax.ppermute(value, "dp", [(i, change(i)) for i in range(shards)])

    got = scatter_cols_start(parts)
    dw = lax.dot_general(
        hidden_attn, grad_proj, (((0,), (0,)), ((), ())), preferred_element_type=F32
    )
    middle = features // 2
    top = jnp.concatenate([dw[:middle], fold_back(dwo[:, :middle])], axis=0)
    bottom = jnp.concatenate([dw[middle:], fold_back(dwo[:, middle:])], axis=0)
    dense_other = exchange(jnp.where(lower, bottom, top).astype(BF16))
    got, dense_other = together((got, dense_other))
    dense = jnp.where(lower, top, bottom) + dense_other.astype(F32)
    kept, got = scatter_cols_next(parts, got)
    dense_other = over_dp(dense.astype(BF16), lambda i: i ^ 1)
    got, dense_other = together((got, dense_other))
    dense = dense + dense_other.astype(F32)
    sent = dense.astype(BF16)
    dense_got = [over_dp(sent, lambda i, k=k: (i + 2 * k) % shards) for k in range(1, shards // 2)]

    sum_a, sum_b = scatter_cols_end(kept, got)
    inner_attn = token_sums(sum_a, sum_b) / features
    grad_hidden = rows_of(sum_a, sum_b)
    normed_attn = inputs * scale_attn
    gain_attn_part = jnp.sum(grad_hidden * normed_attn, axis=0)
    grad_tokens = (
        grad_mid + scale_attn * (grad_hidden * own_gains[0][None, :] - normed_attn * inner_attn)
    ).astype(BF16)
    gain_parts = jnp.stack([gain_attn_part, gain_moe_part])
    gain_other = over_dp(gain_parts, lambda i: i ^ 1)
    sent = jnp.where(lower, grad_tokens[:, HEAD:], grad_tokens[:, :HEAD])
    token_got = exchange(sent)
    gain_other, token_got, weights = together((gain_other, token_got, weights))
    gain_parts = gain_parts + gain_other
    result = (midway + RESID_SCALE * expert_sum).astype(BF16)
    gain_other = over_dp(gain_parts, lambda i: (i + 2) % shards if i // 2 % 2 == 0 else i - 2)
    result_got = exchange(jnp.where(lower, result[:, HEAD:], result[:, :HEAD]))
    gain_other, result_got, dense_got = together((gain_other, result_got, dense_got))
    dense = total([dense, *dense_got])
    gain_parts = gain_parts + gain_other
    gain_parts = gain_parts + over_dp(gain_parts, lambda i: (i + shards // 2) % shards)
    gain_parts = gain_parts + exchange(gain_parts)
    gain_parts = jnp.where(lower, gain_parts[:, :HEAD], gain_parts[:, HEAD:])

    def narrow(value, got):
        own = jnp.where(lower, value[:, :HEAD], value[:, HEAD:])
        return from_halves(jnp.where(lower, own, got), jnp.where(lower, got, own))

    query_width = w_query.shape[1]
    key_width = key_matrix.shape[1]
    dw, dwo = dense[:middle], unfold_back(dense[middle:])
    return (
        narrow(result, result_got),
        narrow(grad_tokens, token_got),
        gain_parts[0],
        gain_parts[1],
        dw[:, :query_width],
        dw[:, query_width : query_width + key_width],
        dw[:, query_width + key_width :],
        dwo,
        *spread(weights),
    )


def solution(mesh):
    return jax.shard_map(
        functools.partial(body, cols=mesh.shape["col"], shards=mesh.shape["dp"]),
        mesh=mesh,
        in_specs=(
            P("dp", ("row", "col")),
            P(("row", "col")),
            P(("row", "col")),
            P("row", "col"),
            P("row", "col"),
            P("row", "col"),
            P("col", "row"),
            P("col", None, "row"),
            P("col", None, "row"),
            P("col", "row", None),
            P("dp", None),
            P("dp", None),
            P("dp", None),
            P("dp", ("row", "col")),
        ),
        out_specs=(
            P("dp", ("row", "col")),
            P("dp", ("row", "col")),
            P(("row", "col")),
            P(("row", "col")),
            P("row", "col"),
            P("row", "col"),
            P("row", "col"),
            P("col", "row"),
            P("col", None, "row"),
            P("col", None, "row"),
            P("col", "row", None),
        ),
        check_vma=False,
    )
```
